32 devices in a mesh: rep: 2 (over x), grp: 8 (over z, y), loc: 2 (over core).
Axes of the slice: x: 2, y: 2, z: 4, core: 2. Of those that a mesh axis runs over, the one named last changes fastest.
Arguments:
- tokens: bfloat16 [4096, 3584], P(('rep', 'grp', 'loc')), parts along dimension 0, may hold values from -6 to 6
- norm_gain: float32 [3584], replicated, may hold values from 0.5 to 1.5
- gate_weight: bfloat16 [8, 3584, 1024], P('grp', 'loc'), may hold values from -0.09375 to 0.09375
- up_weight: bfloat16 [8, 3584, 1024], P('grp', 'loc'), may hold values from -0.09375 to 0.09375
- down_weight: bfloat16 [8, 1024, 3584], P('grp', None, 'loc'), may hold values from -0.1875 to 0.1875
- expert_ids: int32 [4096, 4], P(('rep', 'grp', 'loc')), parts along dimension 0, may hold values from 0 to 7, as said below
- numerators: int32 [4096, 4], P(('rep', 'grp', 'loc')), parts along dimension 0, may hold values from 1 to 128
Outputs:
- moe_out: bfloat16 [4096, 3584], P(('rep', 'grp', 'loc')), parts along dimension 0
The draws below stay inside these ranges and needn't reach their ends.
There are 2 independent parts, one for each index of `rep`. The reference program is written for one: setup_inputs(seed, part) draws one part's arguments, and reference() takes and returns one part's arrays. A program takes and returns all parts, laid end to end along the dimension named above; an argument that names none is the same for every part. Nothing has to cross between parts.
Inputs may be any that keep to these rules, and one draw needn't show every extreme that they name: `expert_ids`: expert e lies in group e // 1. Each token names 4 different experts, one in each of four different groups. In each aligned block of 128 tokens every group is named by exactly half of the tokens, no expert is named by more than 64 tokens, and some expert is named by exactly 64; some experts are named by 64 tokens of every block.
All inputs are finite; a program needn't handle non-finite values.
Results may differ from the reference program's by a relative error of at most 0.015.
Values may be sent and summed in bfloat16 or wider, within the bound.
A program may use at most 64 MiB of HBM per device.

```python
import jax
import jax.numpy as jnp
from jax import lax

D = 3584
FF_WIN = 1024
TOPK = 4
TOK_DEV = 128
EXPERTS = 8
TOKENS = 2048
CAP = 64


def draw_expert_ids(key, part):
    sources = TOKENS // TOK_DEV
    per_group = EXPERTS // 8
    half_tok = TOK_DEV // 2
    hot_member = jax.random.randint(jax.random.fold_in(key, 11), (8,), 0, per_group)
    bounds = jnp.array([9, 17, 25], jnp.int32) * (half_tok // 32)

    def one_source(source_key):
        key_order, key_group, key_offset, key_member = jax.random.split(source_key, 4)
        group_label = jax.random.permutation(key_group, 8)
        token_rank = jax.random.permutation(key_order, TOK_DEV)
        side_index = token_rank // half_tok
        slot_group = group_label[2 * jnp.arange(TOPK)[None, :] + side_index[:, None]]
        offsets = jax.random.randint(key_offset, (TOPK,), 0, half_tok)
        within = (token_rank[:, None] % half_tok + offsets[None, :]) % half_tok
        if per_group > 1:
            member_rank = jnp.sum((within[:, :, None] >= bounds[None, None, :]).astype(jnp.int32), axis=2)
            member_keys = jax.random.split(key_member, 8)
            rest_perm = jax.vmap(lambda member_key: jax.random.permutation(member_key, per_group - 1) + 1)(member_keys)
            shift_table = jnp.concatenate([jnp.zeros((8, 1), jnp.int32), rest_perm.astype(jnp.int32)], axis=1)
            member = (hot_member[slot_group] + shift_table[slot_group, member_rank]) % per_group
        else:
            member = jnp.zeros_like(slot_group)
        return slot_group * per_group + member
    chosen_ids = jax.vmap(one_source)(jax.random.split(jax.random.fold_in(key, 7), sources))
    return chosen_ids.reshape(TOKENS, TOPK).astype(jnp.int32)


def place_ends(values, stream_key, smallest, high):
    dims = values.shape
    place = [jax.random.randint(jax.random.fold_in(stream_key, axis), (), 0, dims[axis]) for axis in range(len(dims))]
    values = values.at[tuple(place)].set(smallest)
    longest = dims.index(max(dims))
    place[longest] = (place[longest] + 1) % dims[longest]
    return values.at[tuple(place)].set(high)


def steps_of(own_key, dims, pieces, smallest, largest):
    def one(position, blocks):
        heights = jax.random.uniform(jax.random.fold_in(jax.random.fold_in(own_key, 6), position), (blocks,), jnp.float32, smallest / len(pieces), largest / len(pieces))
        return jnp.repeat(jnp.exp(heights), dims[position] // blocks).reshape((-1,) + (1,) * (len(dims) - position - 1))

    level = one(*pieces[0])
    for cut in pieces[1:]:
        level = level * one(*cut)
    return level


def bell_draw(rng, dims, spread, limit, shards=(), held_as=jnp.bfloat16):
    result = spread * jax.random.normal(rng, dims, jnp.float32)
    if shards:
        result = result * steps_of(rng, dims, shards, -0.22, 0.18)
    return jnp.clip(result, -limit, limit).astype(held_as)


def setup_inputs(seed: int = 0, part: int = 0) -> dict:
    streams_of = jax.random.split(jax.random.key(seed), 8)
    part_keys = jax.random.split(jax.random.fold_in(streams_of[7], part), 8)
    tokens = bell_draw(part_keys[0], (TOKENS, D), 1.0, 6.0, ((0, 16),))
    norm_gain = jnp.clip(1.0 + 0.1 * jax.random.normal(streams_of[1], (D,), jnp.float32), 0.5, 1.5)
    gate_weight = bell_draw(streams_of[2], (EXPERTS, D, FF_WIN), D ** -0.5, 0.09375, ((0, 8), (1, 2)))
    up_weight = bell_draw(streams_of[3], (EXPERTS, D, FF_WIN), D ** -0.5, 0.09375, ((0, 8), (1, 2)))
    down_weight = bell_draw(streams_of[4], (EXPERTS, FF_WIN, D), FF_WIN ** -0.5, 0.1875, ((0, 8), (2, 2)))
    expert_ids = draw_expert_ids(jax.random.fold_in(jax.random.fold_in(streams_of[7], part), 71), part)
    numerators = place_ends(jax.random.randint(part_keys[6], (TOKENS, TOPK), 1, 129), jax.random.fold_in(part_keys[6], 1), 1, 128).astype(jnp.int32)
    return {"tokens": tokens, "norm_gain": norm_gain, "gate_weight": gate_weight, "up_weight": up_weight, "down_weight": down_weight, "expert_ids": expert_ids, "numerators": numerators}


def rounded(number):
    return lax.optimization_barrier(number.astype(jnp.bfloat16)).astype(jnp.float32)

def expert_rows(rows, w_gate, w_up, w_down):
    half_width = D // 2

    def split_product(weight):
        first_part = jnp.dot(rows[:, :half_width], weight[:half_width], preferred_element_type=jnp.float32)
        second_part = jnp.dot(rows[:, half_width:], weight[half_width:], preferred_element_type=jnp.float32)
        return rounded(first_part) + rounded(second_part)
    gate_sum = split_product(w_gate)
    up_sum = split_product(w_up)
    hidden = (jax.nn.silu(gate_sum) * up_sum).astype(jnp.bfloat16)
    return jnp.dot(hidden, w_down, preferred_element_type=jnp.float32).astype(jnp.bfloat16)

def reference(tokens, norm_gain, gate_weight, up_weight, down_weight, expert_ids, numerators):
    values = tokens.astype(jnp.float32)
    norm_scale = lax.rsqrt(lax.optimization_barrier(jnp.mean(values * values, axis=-1, keepdims=True)) + 1e-06)
    normed = (values * norm_scale * norm_gain.astype(jnp.float32)).astype(jnp.bfloat16)
    sources = TOKENS // TOK_DEV
    pair_ids = expert_ids.reshape(sources, TOK_DEV * TOPK)
    onehot = (pair_ids[:, :, None] == jnp.arange(EXPERTS, dtype=jnp.int32)[None, None, :]).astype(jnp.int32)
    slot_rank = lax.optimization_barrier(jnp.sum((jnp.cumsum(onehot, axis=1) - 1) * onehot, axis=2))
    row_index = (jnp.arange(sources, dtype=jnp.int32)[:, None] * CAP + slot_rank).reshape(-1).astype(jnp.int32)
    token_index = (jnp.arange(TOKENS * TOPK, dtype=jnp.int32) // TOPK).astype(jnp.int32)
    flat_ids = expert_ids.reshape(-1)
    row_table = jnp.full((EXPERTS, sources * CAP), TOKENS, jnp.int32).at[flat_ids, row_index].set(token_index)
    padded = jnp.concatenate([normed, jnp.zeros((1, D), jnp.bfloat16)], axis=0)

    def one_expert(operands):
        rows_of, w_gate, w_up, w_down = operands
        return expert_rows(padded[rows_of], w_gate, w_up, w_down)
    results = lax.map(one_expert, (row_table, gate_weight, up_weight, down_weight))
    picked = results[flat_ids, row_index].astype(jnp.float32).reshape(TOKENS, TOPK, D)
    weights = numerators.astype(jnp.float32) / 128.0
    return lax.optimization_barrier(jnp.sum(picked * weights[:, :, None], axis=1)).astype(jnp.bfloat16)
```

```python
import functools

import jax
import jax.numpy as jnp
from jax import lax
from jax.experimental import pallas as pl
from jax.experimental.pallas import tpu as pltpu
from jax.sharding import PartitionSpec as P


def local(tokens, norm_gain, gate_weight, up_weight, down_weight, expert_ids, numerators):
    tok_count, width = tokens.shape
    chosen = expert_ids.shape[1]
    experts = lax.axis_size("grp")
    halves = lax.axis_size("loc")
    half_width = width // halves
    capacity = tok_count // 2 - experts // 32 * (23 * tok_count // 64)
    values = tokens.astype(jnp.float32)
    norm_scale = lax.rsqrt(jnp.mean(values * values, axis=-1, keepdims=True) + 1e-06)
    normed = (values * norm_scale * norm_gain).astype(jnp.bfloat16)
    flat_ids = expert_ids.reshape(-1)
    onehot = (flat_ids[:, None] == jnp.arange(experts, dtype=jnp.int32)[None, :]).astype(jnp.int32)
    slot_rank = jnp.sum((jnp.cumsum(onehot, axis=0) - 1) * onehot, axis=1)
    target = (flat_ids * capacity + slot_rank).reshape(tok_count, chosen)
    placed = (
        target[:, :, None] == jnp.arange(experts * capacity, dtype=jnp.int32)[None, None, :]
    ).astype(jnp.float32)
    select = jnp.sum(placed, axis=1).astype(jnp.bfloat16).reshape(tok_count, experts, capacity)
    weights = numerators.astype(jnp.float32) / 128.0
    combine = (
        jnp.sum(placed * weights[:, :, None], axis=1)
        .astype(jnp.bfloat16)
        .reshape(tok_count, experts, capacity)
    )
    feature_halves = normed.reshape(tok_count, halves, half_width)
    outgoing = jnp.einsum(
        "tec,thf->ehcf", select, feature_halves, preferred_element_type=jnp.float32
    ).astype(jnp.bfloat16)
    arrived = lax.all_to_all(
        outgoing.reshape(experts * halves, capacity, half_width),
        ("grp", "loc"),
        split_axis=0,
        concat_axis=0,
        tiled=True,
    )
    expert_input = arrived.reshape(-1, half_width)
    gate_part = jnp.dot(expert_input, gate_weight[0], preferred_element_type=jnp.float32)
    up_part = jnp.dot(expert_input, up_weight[0], preferred_element_type=jnp.float32)
    down_local = down_weight[0]
    gate_sum, up_sum = (
        lax.psum(gate_part.astype(jnp.bfloat16), "loc").astype(jnp.float32),
        lax.psum(up_part.astype(jnp.bfloat16), "loc").astype(jnp.float32),
    )
    hidden_all = (jax.nn.silu(gate_sum) * up_sum).astype(jnp.bfloat16)
    expert_out = jnp.dot(hidden_all, down_local, preferred_element_type=jnp.float32)
    expert_out = expert_out.astype(jnp.bfloat16)
    returned = lax.all_to_all(
        expert_out.reshape(experts * halves, capacity, half_width),
        ("grp", "loc"),
        split_axis=0,
        concat_axis=0,
        tiled=True,
    ).reshape(experts, halves, capacity, half_width)
    mixed = jnp.einsum("tec,ehcf->thf", combine, returned, preferred_element_type=jnp.float32)
    return mixed.reshape(tok_count, width).astype(jnp.bfloat16)


def chain_kernel(
    lanes, steps, cap,
    tok_ref, gain_ref, ids_ref, num_ref, gate_hbm, up_hbm, down_hbm, out_ref,
    gate_w, up_w, down_w, stage, gathered, meta, cross, rows, part, part_in, made, back, total, total_in, last, last_in,
    weight_sem, pair_send, pair_recv, pair_meta_send, pair_meta_recv, hop_send, hop_recv, meta_send, meta_recv,
    cross_send, cross_recv, part_send, part_recv, back_send, back_recv, sum_send, sum_recv, last_send, last_recv,
):
    tok_count, width = tok_ref.shape
    half_width = width // 2
    hidden_width = gate_w.shape[1]
    experts = lanes * steps
    group = lax.axis_index("grp")
    core = lax.axis_index("loc")
    place = group // lanes
    lane = group % lanes
    other_core = 1 - core
    other_lane = place * lanes + 1 - lane
    left, right = group - lanes, group + lanes
    has_left, has_right = place > 0, place < steps - 1
    mesh_id = pl.DeviceIdType.MESH

    def remote(src, dst, send, recv, target):
        return pltpu.make_async_remote_copy(
            src_ref=src, dst_ref=dst, send_sem=send, recv_sem=recv, device_id=target, device_id_type=mesh_id
        )

    weight_copies = [
        pltpu.make_async_copy(src.at[0], dst, weight_sem.at[k])
        for k, (src, dst) in enumerate(((gate_hbm, gate_w), (up_hbm, up_w), (down_hbm, down_w)))
    ]
    for copy in weight_copies:
        copy.start()

    barrier = pltpu.get_barrier_semaphore()
    pl.semaphore_signal(barrier, inc=1, device_id={"loc": other_core}, device_id_type=mesh_id)
    pl.semaphore_signal(barrier, inc=1, device_id={"grp": other_lane}, device_id_type=mesh_id)

    @pl.when(has_left)
    def _():
        pl.semaphore_signal(barrier, inc=1, device_id={"grp": left}, device_id_type=mesh_id)

    @pl.when(has_right)
    def _():
        pl.semaphore_signal(barrier, inc=1, device_id={"grp": right}, device_id_type=mesh_id)

    expert_row = lax.broadcasted_iota(jnp.int32, (experts, tok_count), 0)
    named = jnp.zeros((experts, tok_count), jnp.float32)
    weight = jnp.zeros((experts, tok_count), jnp.float32)
    for k in range(ids_ref.shape[0]):
        hit = ids_ref[k : k + 1, :] == expert_row
        named = named + jnp.where(hit, 1.0, 0.0)
        weight = weight + jnp.where(hit, num_ref[k : k + 1, :].astype(jnp.float32) / 128.0, 0.0)
    earlier = lax.broadcasted_iota(jnp.int32, (tok_count, tok_count), 0) < lax.broadcasted_iota(
        jnp.int32, (tok_count, tok_count), 1
    )
    slot = jnp.dot(
        named.astype(jnp.bfloat16),
        jnp.where(earlier, 1.0, 0.0).astype(jnp.bfloat16),
        preferred_element_type=jnp.float32,
    )
    meta[place, core, 0:experts, :] = jnp.where(named > 0.5, slot, -1.0)
    meta[place, core, experts : 2 * experts, :] = weight

    values = tok_ref[...].astype(jnp.float32)
    scale = lax.rsqrt(jnp.mean(values * values, axis=-1, keepdims=True) + 1e-06)

    def normed(which):
        cols = pl.ds(pl.multiple_of(which * half_width, 128), half_width)
        return (tok_ref[:, cols].astype(jnp.float32) * scale * gain_ref[:, cols]).astype(jnp.bfloat16)

    stage[...] = normed(other_core)
    pl.semaphore_wait(barrier, 2 + has_left.astype(jnp.int32) + has_right.astype(jnp.int32))
    own = (place, core)
    pair_copies = [
        remote(stage, gathered.at[own], pair_send, pair_recv, {"loc": other_core}),
        remote(meta.at[own], meta.at[own], pair_meta_send, pair_meta_recv, {"loc": other_core}),
    ]
    for copy in pair_copies:
        copy.start()
    gathered[place, core] = normed(core)
    for copy in pair_copies:
        copy.wait_send()

    def hop(b, h, side):
        target = {"grp": (left, right)[side]}
        return (
            remote(gathered.at[b, h], gathered.at[b, h], hop_send.at[side, b, h], hop_recv.at[b, h], target),
            remote(meta.at[b, h], meta.at[b, h], meta_send.at[side, b, h], meta_recv.at[b, h], target),
        )

    def start_hop(b, h, side):
        for copy in hop(b, h, side):
            copy.start()

    def forward(i):
        h, d = i // steps, i % steps

        @pl.when(d == 0)
        def _():
            @pl.when(h != core)
            def _():
                got = (place, other_core)
                remote(stage, gathered.at[got], pair_send, pair_recv, {"loc": other_core}).wait_recv()
                remote(meta.at[got], meta.at[got], pair_meta_send, pair_meta_recv, {"loc": other_core}).wait_recv()

            @pl.when(has_left)
            def _():
                start_hop(place, h, 0)

            @pl.when(has_right)
            def _():
                start_hop(place, h, 1)

        @pl.when((d > 0) & (place - d >= 0))
        def _():
            for copy in hop(place - d, h, 1):
                copy.wait_recv()

            @pl.when(has_right)
            def _():
                start_hop(place - d, h, 1)

        @pl.when((d > 0) & (place + d < steps))
        def _():
            for copy in hop(place + d, h, 0):
                copy.wait_recv()

            @pl.when(has_left)
            def _():
                start_hop(place + d, h, 0)

    def chunk(i):
        h, j = i // steps, i % steps
        near = jnp.minimum(place, steps - 1 - place)
        both = j <= 2 * near
        d = jnp.where(both, (j + 1) // 2, j - near)
        up = jnp.where(both, j % 2 == 0, place < steps - 1 - place)
        return jnp.where(up, place + d, place - d), h

    slot_row = lax.broadcasted_iota(jnp.int32, (cap, tok_count), 0).astype(jnp.float32)

    def table(b, h, expert):
        return meta[b, h, pl.ds(expert, 1), :] == slot_row

    def weighted(b, h, expert):
        return jnp.where(table(b, h, expert), meta[b, h, pl.ds(experts + expert, 1), :], 0.0).astype(jnp.bfloat16)

    def pick(b, h, expert):
        chosen = jnp.where(table(b, h, expert), 1.0, 0.0).astype(jnp.bfloat16)
        return jnp.dot(chosen, gathered[b, h], preferred_element_type=jnp.float32).astype(jnp.bfloat16)

    def cross_copy(b, h):
        return remote(
            cross.at[b, h], rows.at[b, h, pl.ds(cap, cap)], cross_send.at[b, h], cross_recv.at[b, h], {"grp": other_lane}
        )

    def part_copy(b, h):
        return remote(part.at[b, h], part_in.at[b, h], part_send.at[b, h], part_recv.at[b, h], {"loc": other_core})

    def back_copy(b, h):
        return remote(
            made.at[b, h, pl.ds(cap, cap)], back.at[b, h], back_send.at[b, h], back_recv.at[b, h], {"grp": other_lane}
        )

    def sum_copy(b, h, side):
        return remote(
            total.at[b, h],
            total_in.at[side, b, h],
            sum_send.at[b, h],
            sum_recv.at[side, b, h],
            {"grp": (left, right)[side]},
        )

    def select(b, h):
        cross[b, h] = pick(b, h, other_lane)
        cross_copy(b, h).start()
        rows[b, h, 0:cap, :] = pick(b, h, group)

    def experts_of(b, h):
        cross_copy(b, h).wait_recv()
        for k, w in enumerate((gate_w, up_w)):
            part[b, h, :, k * hidden_width : (k + 1) * hidden_width] = jnp.dot(
                rows[b, h], w[...], preferred_element_type=jnp.float32
            ).astype(jnp.bfloat16)
        part_copy(b, h).start()
        part_copy(b, h).wait_recv()
        both = part[b, h].astype(jnp.float32) + part_in[b, h].astype(jnp.float32)
        gate_sum, up_sum = both[:, :hidden_width], both[:, hidden_width:]
        hidden = (gate_sum / (1.0 + jnp.exp(-gate_sum)) * up_sum).astype(jnp.bfloat16)
        made[b, h] = jnp.dot(hidden, down_w[...], preferred_element_type=jnp.float32).astype(jnp.bfloat16)
        back_copy(b, h).start()

    def combine(b, h):
        back_copy(b, h).wait_recv()
        dims = (((0,), (0,)), ((), ()))
        total[b, h] = (
            lax.dot_general(weighted(b, h, group), made[b, h, 0:cap, :], dims, preferred_element_type=jnp.float32)
            + lax.dot_general(weighted(b, h, other_lane), back[b, h], dims, preferred_element_type=jnp.float32)
        ).astype(jnp.bfloat16)

        @pl.when((b > place) & jnp.logical_not(has_left))
        def _():
            sum_copy(b, h, 1).start()

        @pl.when((b < place) & jnp.logical_not(has_right))
        def _():
            sum_copy(b, h, 0).start()

    def add_in(b, h, side):
        sum_copy(b, h, side).wait_recv()
        total[b, h] = (total[b, h].astype(jnp.float32) + total_in[side, b, h].astype(jnp.float32)).astype(jnp.bfloat16)

    def reduce_step(i):
        for h in range(2):
            going_right = i - h * steps - 2 * place
            going_left = steps - 1 - (i - h * steps - 2 * (steps - 1 - place))

            @pl.when(has_left & (going_right > place) & (going_right < steps))
            def _():
                add_in(going_right, h, 1)
                sum_copy(going_right, h, 1).start()

            @pl.when(has_right & (going_left < place) & (going_left >= 0))
            def _():
                add_in(going_left, h, 0)
                sum_copy(going_left, h, 0).start()

    def body(i, carry):
        @pl.when(i < 2 * steps)
        def _():
            forward(i)
            select(*chunk(i))

        reduce_step(i)

        @pl.when((i >= 1) & (i <= 2 * steps))
        def _():
            combine(*chunk(i - 1))

        @pl.when(i == 0)
        def _():
            for copy in weight_copies:
                copy.wait()

        @pl.when(i < 2 * steps)
        def _():
            experts_of(*chunk(i))

        return carry

    lax.fori_loop(0, max(4 * steps - 4, 2 * steps + 1), body, 0)

    def finish(h):
        @pl.when(has_left)
        def _():
            add_in(place, h, 1)

        @pl.when(has_right)
        def _():
            add_in(place, h, 0)

    last_copy = remote(last, last_in, last_send, last_recv, {"loc": other_core})
    for h in range(2):
        finish(h)

        @pl.when(h != core)
        def _():
            last[...] = total[place, h]
            last_copy.start()

        @pl.when(h == core)
        def _():
            out_ref[:, pl.ds(pl.multiple_of(core * half_width, 128), half_width)] = total[place, h]

    last_copy.wait()
    out_ref[:, pl.ds(pl.multiple_of(other_core * half_width, 128), half_width)] = last_in[...]

    def drain(i, carry):
        b, h = i // 2, i % 2

        @pl.when((b <= place) & has_right)
        def _():
            for copy in hop(b, h, 1):
                copy.wait_send()

        @pl.when((b >= place) & has_left)
        def _():
            for copy in hop(b, h, 0):
                copy.wait_send()

        cross_copy(b, h).wait_send()
        part_copy(b, h).wait_send()
        back_copy(b, h).wait_send()

        @pl.when(b != place)
        def _():
            sum_copy(b, h, 0).wait_send()

        return carry

    lax.fori_loop(0, 2 * steps, drain, 0)


def chained(tokens, norm_gain, gate_weight, up_weight, down_weight, expert_ids, numerators):
    tok_count, width = tokens.shape
    experts = lax.axis_size("grp")
    half_width = width // 2
    hidden_width = gate_weight.shape[2]
    lanes = 2
    steps = experts // lanes
    cap = capacity_of(tok_count, experts)
    bf = jnp.bfloat16
    dma = pltpu.SemaphoreType.DMA
    vmem = pl.BlockSpec(memory_space=pltpu.VMEM)
    hbm = pl.BlockSpec(memory_space=pl.ANY)
    return pl.pallas_call(
        functools.partial(chain_kernel, lanes, steps, cap),
        out_shape=jax.ShapeDtypeStruct((tok_count, width), bf),
        in_specs=[vmem, vmem, vmem, vmem, hbm, hbm, hbm],
        out_specs=vmem,
        scratch_shapes=[
            pltpu.VMEM((half_width, hidden_width), bf),
            pltpu.VMEM((half_width, hidden_width), bf),
            pltpu.VMEM((hidden_width, half_width), bf),
            pltpu.VMEM((tok_count, half_width), bf),
            pltpu.VMEM((steps, 2, tok_count, half_width), bf),
            pltpu.VMEM((steps, 2, 2 * experts, tok_count), jnp.float32),
            pltpu.VMEM((steps, 2, cap, half_width), bf),
            pltpu.VMEM((steps, 2, 2 * cap, half_width), bf),
            pltpu.VMEM((steps, 2, 2 * cap, 2 * hidden_width), bf),
            pltpu.VMEM((steps, 2, 2 * cap, 2 * hidden_width), bf),
            pltpu.VMEM((steps, 2, 2 * cap, half_width), bf),
            pltpu.VMEM((steps, 2, cap, half_width), bf),
            pltpu.VMEM((steps, 2, tok_count, half_width), bf),
            pltpu.VMEM((2, steps, 2, tok_count, half_width), bf),
            pltpu.VMEM((tok_count, half_width), bf),
            pltpu.VMEM((tok_count, half_width), bf),
            dma((3,)),
            dma, dma, dma, dma,
            dma((2, steps, 2)), dma((steps, 2)), dma((2, steps, 2)), dma((steps, 2)),
            dma((steps, 2)), dma((steps, 2)), dma((steps, 2)), dma((steps, 2)),
            dma((steps, 2)), dma((steps, 2)), dma((steps, 2)), dma((2, steps, 2)),
            dma, dma,
        ],
        compiler_params=pltpu.CompilerParams(
            collective_id=0, has_side_effects=True, vmem_limit_bytes=60 * 1024 * 1024
        ),
    )(tokens, norm_gain[None, :], expert_ids.T, numerators.T, gate_weight, up_weight, down_weight)


def capacity_of(tok_count, experts):
    return tok_count // 2 - experts // 32 * (23 * tok_count // 64)


def solution(mesh):
    in_specs = (
        P(("rep", "grp", "loc"), None),
        P(),
        P("grp", "loc", None),
        P("grp", "loc", None),
        P("grp", None, "loc"),
        P(("rep", "grp", "loc"), None),
        P(("rep", "grp", "loc"), None),
    )
    out_specs = P(("rep", "grp", "loc"), None)
    experts, halves = mesh.shape["grp"], mesh.shape["loc"]

    def run(tokens, *rest):
        tok_count = tokens.shape[0] // mesh.size
        whole_tiles = capacity_of(tok_count, experts) % 16 == 0 and experts % 8 == 0 and halves == 2
        return jax.shard_map(
            chained if whole_tiles else local, mesh=mesh, in_specs=in_specs, out_specs=out_specs, check_vma=False
        )(tokens, *rest)

    return run
```

```python
import functools

import jax
import jax.numpy as jnp
from jax import lax
from jax.experimental import pallas as pl
from jax.experimental.pallas import tpu as pltpu
from jax.sharding import PartitionSpec as P


def local(tokens, norm_gain, gate_weight, up_weight, down_weight, expert_ids, numerators):
    tok_count, width = tokens.shape
    chosen = expert_ids.shape[1]
    experts = lax.axis_size("grp")
    halves = lax.axis_size("loc")
    half_width = width // halves
    capacity = tok_count // 2 - experts // 32 * (23 * tok_count // 64)
    values = tokens.astype(jnp.float32)
    norm_scale = lax.rsqrt(jnp.mean(values * values, axis=-1, keepdims=True) + 1e-06)
    normed = (values * norm_scale * norm_gain).astype(jnp.bfloat16)
    flat_ids = expert_ids.reshape(-1)
    onehot = (flat_ids[:, None] == jnp.arange(experts, dtype=jnp.int32)[None, :]).astype(jnp.int32)
    slot_rank = jnp.sum((jnp.cumsum(onehot, axis=0) - 1) * onehot, axis=1)
    target = (flat_ids * capacity + slot_rank).reshape(tok_count, chosen)
    placed = (
        target[:, :, None] == jnp.arange(experts * capacity, dtype=jnp.int32)[None, None, :]
    ).astype(jnp.float32)
    select = jnp.sum(placed, axis=1).astype(jnp.bfloat16).reshape(tok_count, experts, capacity)
    weights = numerators.astype(jnp.float32) / 128.0
    combine = (
        jnp.sum(placed * weights[:, :, None], axis=1)
        .astype(jnp.bfloat16)
        .reshape(tok_count, experts, capacity)
    )
    feature_halves = normed.reshape(tok_count, halves, half_width)
    outgoing = jnp.einsum(
        "tec,thf->ehcf", select, feature_halves, preferred_element_type=jnp.float32
    ).astype(jnp.bfloat16)
    arrived = lax.all_to_all(
        outgoing.reshape(experts * halves, capacity, half_width),
        ("grp", "loc"),
        split_axis=0,
        concat_axis=0,
        tiled=True,
    )
    expert_input = arrived.reshape(-1, half_width)
    gate_part = jnp.dot(expert_input, gate_weight[0], preferred_element_type=jnp.float32)
    up_part = jnp.dot(expert_input, up_weight[0], preferred_element_type=jnp.float32)
    down_local = down_weight[0]
    gate_sum, up_sum = (
        lax.psum(gate_part.astype(jnp.bfloat16), "loc").astype(jnp.float32),
        lax.psum(up_part.astype(jnp.bfloat16), "loc").astype(jnp.float32),
    )
    hidden_all = (jax.nn.silu(gate_sum) * up_sum).astype(jnp.bfloat16)
    expert_out = jnp.dot(hidden_all, down_local, preferred_element_type=jnp.float32)
    expert_out = expert_out.astype(jnp.bfloat16)
    returned = lax.all_to_all(
        expert_out.reshape(experts * halves, capacity, half_width),
        ("grp", "loc"),
        split_axis=0,
        concat_axis=0,
        tiled=True,
    ).reshape(experts, halves, capacity, half_width)
    mixed = jnp.einsum("tec,ehcf->thf", combine, returned, preferred_element_type=jnp.float32)
    return mixed.reshape(tok_count, width).astype(jnp.bfloat16)


def chain_kernel(
    lanes, steps, cap,
    tok_ref, gain_ref, ids_ref, num_ref, gate_hbm, up_hbm, down_hbm, out_ref,
    gate_w, up_w, down_w, stage, gathered, meta, cross, rows, part, part_in, made, back, total, total_in, last, last_in,
    weight_sem, pair_send, pair_recv, pair_meta_send, pair_meta_recv, hop_send, hop_recv, meta_send, meta_recv,
    cross_send, cross_recv, part_send, part_recv, back_send, back_recv, sum_send, sum_recv, last_send, last_recv,
):
    tok_count, width = tok_ref.shape
    half_width = width // 2
    hidden_width = gate_w.shape[1]
    experts = lanes * steps
    half_tok = tok_count // 2
    group = lax.axis_index("grp")
    core = lax.axis_index("loc")
    place = group // lanes
    lane = group % lanes
    other_core = 1 - core
    other_lane = place * lanes + 1 - lane
    left, right = group - lanes, group + lanes
    has_left, has_right = place > 0, place < steps - 1
    mesh_id = pl.DeviceIdType.MESH

    def remote(src, dst, send, recv, target):
        return pltpu.make_async_remote_copy(
            src_ref=src, dst_ref=dst, send_sem=send, recv_sem=recv, device_id=target, device_id_type=mesh_id
        )

    weight_copies = [
        pltpu.make_async_copy(src.at[0], dst, weight_sem.at[k])
        for k, (src, dst) in enumerate(((gate_hbm, gate_w), (up_hbm, up_w), (down_hbm, down_w)))
    ]
    for copy in weight_copies:
        copy.start()

    barrier = pltpu.get_barrier_semaphore()
    pl.semaphore_signal(barrier, inc=1, device_id={"loc": other_core}, device_id_type=mesh_id)
    pl.semaphore_signal(barrier, inc=1, device_id={"grp": other_lane}, device_id_type=mesh_id)

    @pl.when(has_left)
    def _():
        pl.semaphore_signal(barrier, inc=1, device_id={"grp": left}, device_id_type=mesh_id)

    @pl.when(has_right)
    def _():
        pl.semaphore_signal(barrier, inc=1, device_id={"grp": right}, device_id_type=mesh_id)

    expert_row = lax.broadcasted_iota(jnp.int32, (experts, tok_count), 0)
    named = jnp.zeros((experts, tok_count), jnp.float32)
    weight = jnp.zeros((experts, tok_count), jnp.float32)
    for k in range(ids_ref.shape[0]):
        hit = ids_ref[k : k + 1, :] == expert_row
        named = named + jnp.where(hit, 1.0, 0.0)
        weight = weight + jnp.where(hit, num_ref[k : k + 1, :].astype(jnp.float32) / 128.0, 0.0)
    earlier = lax.broadcasted_iota(jnp.int32, (tok_count, tok_count), 0) < lax.broadcasted_iota(
        jnp.int32, (tok_count, tok_count), 1
    )
    slot = jnp.dot(
        named.astype(jnp.bfloat16),
        jnp.where(earlier, 1.0, 0.0).astype(jnp.bfloat16),
        preferred_element_type=jnp.float32,
    )
    meta[place, core, 0:experts, :] = jnp.where(named > 0.5, slot, -1.0)
    meta[place, core, experts : 2 * experts, :] = weight

    values = tok_ref[...].astype(jnp.float32)
    scale = lax.rsqrt(jnp.mean(values * values, axis=-1, keepdims=True) + 1e-06)

    def normed(which):
        cols = pl.ds(pl.multiple_of(which * half_width, 128), half_width)
        return (tok_ref[:, cols].astype(jnp.float32) * scale * gain_ref[:, cols]).astype(jnp.bfloat16)

    stage[...] = normed(other_core)
    pl.semaphore_wait(barrier, 2 + has_left.astype(jnp.int32) + has_right.astype(jnp.int32))
    own = (place, core)
    pair_copies = [
        remote(stage, gathered.at[own], pair_send, pair_recv, {"loc": other_core}),
        remote(meta.at[own], meta.at[own], pair_meta_send, pair_meta_recv, {"loc": other_core}),
    ]
    for copy in pair_copies:
        copy.start()
    gathered[place, core] = normed(core)
    for copy in pair_copies:
        copy.wait_send()
    got = (place, other_core)
    remote(stage, gathered.at[got], pair_send, pair_recv, {"loc": other_core}).wait_recv()
    remote(meta.at[got], meta.at[got], pair_meta_send, pair_meta_recv, {"loc": other_core}).wait_recv()

    def hop(b, h, side):
        target = {"grp": (left, right)[side]}
        return (
            remote(gathered.at[b, h], gathered.at[b, h], hop_send.at[side, b, h], hop_recv.at[b, h], target),
            remote(meta.at[b, h], meta.at[b, h], meta_send.at[side, b, h], meta_recv.at[b, h], target),
        )

    def start_hop(b, h, side):
        for copy in hop(b, h, side):
            copy.start()

    def forward_one(i, upstream, sign, side, has_next):
        first = i <= upstream
        d = jnp.where(first, i, 2 * upstream + 1 - i)
        b, h = place + sign * d, jnp.where(first, 0, 1)

        @pl.when(d >= 0)
        def _():
            @pl.when(d > 0)
            def _():
                for copy in hop(b, h, side):
                    copy.wait_recv()

            @pl.when(has_next)
            def _():
                start_hop(b, h, side)

    def forward(i):
        forward_one(i, steps - 1 - place, 1, 0, has_left)
        forward_one(i, place, -1, 1, has_right)

    def chunk(i):
        h = i // steps
        j = jnp.where(h == 0, i, 2 * steps - 1 - i)
        near = jnp.minimum(place, steps - 1 - place)
        both = j <= 2 * near
        d = jnp.where(both, (j + 1) // 2, j - near)
        up = jnp.where(both, j % 2 == 0, place < steps - 1 - place)
        return jnp.where(up, place + d, place - d), h

    slot_row = lax.broadcasted_iota(jnp.int32, (cap, tok_count), 0).astype(jnp.float32)

    def table(b, h, expert):
        return meta[b, h, pl.ds(expert, 1), :] == slot_row

    def weighted(b, h, expert):
        return jnp.where(table(b, h, expert), meta[b, h, pl.ds(experts + expert, 1), :], 0.0).astype(jnp.bfloat16)

    def pick(b, h, expert):
        chosen = jnp.where(table(b, h, expert), 1.0, 0.0).astype(jnp.bfloat16)
        return jnp.dot(chosen, gathered[b, h], preferred_element_type=jnp.float32).astype(jnp.bfloat16)

    def cross_copy(b, h):
        return remote(
            cross.at[b, h], rows.at[b, h, pl.ds(cap, cap)], cross_send.at[b, h], cross_recv.at[b, h], {"grp": other_lane}
        )

    def part_copy(b, h):
        return remote(part.at[b, h], part_in.at[b, h], part_send.at[b, h], part_recv.at[b, h], {"loc": other_core})

    def back_copy(b, h):
        return remote(
            made.at[b, h, pl.ds(cap, cap)], back.at[b, h], back_send.at[b, h], back_recv.at[b, h], {"grp": other_lane}
        )

    def sum_copy(b, h, side, p):
        at = pl.ds(p * half_tok, half_tok)
        return remote(
            total.at[b, h, at],
            total_in.at[side, b, h, at],
            sum_send.at[b, h, p],
            sum_recv.at[side, b, h, p],
            {"grp": (left, right)[side]},
        )

    def select(b, h):
        cross[b, h] = pick(b, h, other_lane)
        cross_copy(b, h).start()
        rows[b, h, 0:cap, :] = pick(b, h, group)

    def gate_up(b, h):
        cross_copy(b, h).wait_recv()
        for k, w in enumerate((gate_w, up_w)):
            part[b, h, :, k * hidden_width : (k + 1) * hidden_width] = jnp.dot(
                rows[b, h], w[...], preferred_element_type=jnp.float32
            ).astype(jnp.bfloat16)
        part_copy(b, h).start()

    def down(b, h):
        part_copy(b, h).wait_recv()
        both = part[b, h].astype(jnp.float32) + part_in[b, h].astype(jnp.float32)
        gate_sum, up_sum = both[:, :hidden_width], both[:, hidden_width:]
        hidden = (gate_sum / (1.0 + jnp.exp(-gate_sum)) * up_sum).astype(jnp.bfloat16)
        made[b, h] = jnp.dot(hidden, down_w[...], preferred_element_type=jnp.float32).astype(jnp.bfloat16)
        back_copy(b, h).start()

    def combine(b, h):
        back_copy(b, h).wait_recv()
        dims = (((0,), (0,)), ((), ()))
        total[b, h] = (
            lax.dot_general(weighted(b, h, group), made[b, h, 0:cap, :], dims, preferred_element_type=jnp.float32)
            + lax.dot_general(weighted(b, h, other_lane), back[b, h], dims, preferred_element_type=jnp.float32)
        ).astype(jnp.bfloat16)

        @pl.when((b > place) & jnp.logical_not(has_left))
        def _():
            for p in range(2):
                sum_copy(b, h, 1, p).start()

        @pl.when((b < place) & jnp.logical_not(has_right))
        def _():
            for p in range(2):
                sum_copy(b, h, 0, p).start()

    def add_in(b, h, side, p):
        sum_copy(b, h, side, p).wait_recv()
        at = pl.ds(p * half_tok, half_tok)
        total[b, h, at] = (
            total[b, h, at].astype(jnp.float32) + total_in[side, b, h, at].astype(jnp.float32)
        ).astype(jnp.bfloat16)

    def add_on(b, h, side):
        for p in range(2):
            add_in(b, h, side, p)
            sum_copy(b, h, side, p).start()

    def reduce_step(i):
        for h in range(2):
            since_right = i - 2 - 2 * place
            since_left = i - 2 - 2 * (steps - 1 - place)
            if h == 0:
                going_right, going_left = since_right, steps - 1 - since_left
            else:
                going_right, going_left = 2 * steps - 1 - since_right, since_left - steps

            @pl.when(has_left & (going_right > place) & (going_right < steps))
            def _():
                add_on(going_right, h, 1)

            @pl.when(has_right & (going_left < place) & (going_left >= 0))
            def _():
                add_on(going_left, h, 0)

    def body(i, carry):
        @pl.when(i < 2 * steps)
        def _():
            forward(i)
            select(*chunk(i))

        @pl.when(i == 0)
        def _():
            for copy in weight_copies:
                copy.wait()

        @pl.when((i >= 1) & (i <= 2 * steps))
        def _():
            gate_up(*chunk(i - 1))

        @pl.when((i >= 2) & (i <= 2 * steps + 1))
        def _():
            combine(*chunk(i - 2))

        reduce_step(i)

        @pl.when((i >= 1) & (i <= 2 * steps))
        def _():
            down(*chunk(i - 1))

        return carry

    lax.fori_loop(0, max(3 * steps - 1, 2 * steps + 2), body, 0)

    def finish(h):
        @pl.when(has_left)
        def _():
            for p in range(2):
                add_in(place, h, 1, p)

        @pl.when(has_right)
        def _():
            for p in range(2):
                add_in(place, h, 0, p)

    last_copy = remote(last, last_in, last_send, last_recv, {"loc": other_core})
    for h in range(2):
        finish(h)

        @pl.when(h != core)
        def _():
            last[...] = total[place, h]
            last_copy.start()

        @pl.when(h == core)
        def _():
            out_ref[:, pl.ds(pl.multiple_of(core * half_width, 128), half_width)] = total[place, h]

    last_copy.wait()
    out_ref[:, pl.ds(pl.multiple_of(other_core * half_width, 128), half_width)] = last_in[...]

    def drain(i, carry):
        b, h = i // 2, i % 2

        @pl.when((b <= place) & has_right)
        def _():
            for copy in hop(b, h, 1):
                copy.wait_send()

        @pl.when((b >= place) & has_left)
        def _():
            for copy in hop(b, h, 0):
                copy.wait_send()

        cross_copy(b, h).wait_send()
        part_copy(b, h).wait_send()
        back_copy(b, h).wait_send()

        @pl.when(b != place)
        def _():
            for p in range(2):
                sum_copy(b, h, 0, p).wait_send()

        return carry

    lax.fori_loop(0, 2 * steps, drain, 0)


def chained(tokens, norm_gain, gate_weight, up_weight, down_weight, expert_ids, numerators):
    tok_count, width = tokens.shape
    experts = lax.axis_size("grp")
    half_width = width // 2
    hidden_width = gate_weight.shape[2]
    lanes = 2
    steps = experts // lanes
    cap = capacity_of(tok_count, experts)
    bf = jnp.bfloat16
    dma = pltpu.SemaphoreType.DMA
    vmem = pl.BlockSpec(memory_space=pltpu.VMEM)
    hbm = pl.BlockSpec(memory_space=pl.ANY)
    return pl.pallas_call(
        functools.partial(chain_kernel, lanes, steps, cap),
        out_shape=jax.ShapeDtypeStruct((tok_count, width), bf),
        in_specs=[vmem, vmem, vmem, vmem, hbm, hbm, hbm],
        out_specs=vmem,
        scratch_shapes=[
            pltpu.VMEM((half_width, hidden_width), bf),
            pltpu.VMEM((half_width, hidden_width), bf),
            pltpu.VMEM((hidden_width, half_width), bf),
            pltpu.VMEM((tok_count, half_width), bf),
            pltpu.VMEM((steps, 2, tok_count, half_width), bf),
            pltpu.VMEM((steps, 2, 2 * experts, tok_count), jnp.float32),
            pltpu.VMEM((steps, 2, cap, half_width), bf),
            pltpu.VMEM((steps, 2, 2 * cap, half_width), bf),
            pltpu.VMEM((steps, 2, 2 * cap, 2 * hidden_width), bf),
            pltpu.VMEM((steps, 2, 2 * cap, 2 * hidden_width), bf),
            pltpu.VMEM((steps, 2, 2 * cap, half_width), bf),
            pltpu.VMEM((steps, 2, cap, half_width), bf),
            pltpu.VMEM((steps, 2, tok_count, half_width), bf),
            pltpu.VMEM((2, steps, 2, tok_count, half_width), bf),
            pltpu.VMEM((tok_count, half_width), bf),
            pltpu.VMEM((tok_count, half_width), bf),
            dma((3,)),
            dma, dma, dma, dma,
            dma((2, steps, 2)), dma((steps, 2)), dma((2, steps, 2)), dma((steps, 2)),
            dma((steps, 2)), dma((steps, 2)), dma((steps, 2)), dma((steps, 2)),
            dma((steps, 2)), dma((steps, 2)), dma((steps, 2, 2)), dma((2, steps, 2, 2)),
            dma, dma,
        ],
        compiler_params=pltpu.CompilerParams(
            collective_id=0, has_side_effects=True, vmem_limit_bytes=60 * 1024 * 1024
        ),
    )(tokens, norm_gain[None, :], expert_ids.T, numerators.T, gate_weight, up_weight, down_weight)


def capacity_of(tok_count, experts):
    return tok_count // 2 - experts // 32 * (23 * tok_count // 64)


def solution(mesh):
    in_specs = (
        P(("rep", "grp", "loc"), None),
        P(),
        P("grp", "loc", None),
        P("grp", "loc", None),
        P("grp", None, "loc"),
        P(("rep", "grp", "loc"), None),
        P(("rep", "grp", "loc"), None),
    )
    out_specs = P(("rep", "grp", "loc"), None)
    experts, halves = mesh.shape["grp"], mesh.shape["loc"]

    def run(tokens, *rest):
        tok_count = tokens.shape[0] // mesh.size
        whole_tiles = capacity_of(tok_count, experts) % 16 == 0 and experts % 8 == 0 and halves == 2
        return jax.shard_map(
            chained if whole_tiles else local, mesh=mesh, in_specs=in_specs, out_specs=out_specs, check_vma=False
        )(tokens, *rest)

    return run
```

```python
import functools

import jax
import jax.numpy as jnp
from jax import lax
from jax.experimental import pallas as pl
from jax.experimental.pallas import tpu as pltpu
from jax.sharding import PartitionSpec as P


def local(tokens, norm_gain, gate_weight, up_weight, down_weight, expert_ids, numerators):
    tok_count, width = tokens.shape
    chosen = expert_ids.shape[1]
    experts = lax.axis_size("grp")
    halves = lax.axis_size("loc")
    half_width = width // halves
    capacity = tok_count // 2 - experts // 32 * (23 * tok_count // 64)
    values = tokens.astype(jnp.float32)
    norm_scale = lax.rsqrt(jnp.mean(values * values, axis=-1, keepdims=True) + 1e-06)
    normed = (values * norm_scale * norm_gain).astype(jnp.bfloat16)
    flat_ids = expert_ids.reshape(-1)
    onehot = (flat_ids[:, None] == jnp.arange(experts, dtype=jnp.int32)[None, :]).astype(jnp.int32)
    slot_rank = jnp.sum((jnp.cumsum(onehot, axis=0) - 1) * onehot, axis=1)
    target = (flat_ids * capacity + slot_rank).reshape(tok_count, chosen)
    placed = (
        target[:, :, None] == jnp.arange(experts * capacity, dtype=jnp.int32)[None, None, :]
    ).astype(jnp.float32)
    select = jnp.sum(placed, axis=1).astype(jnp.bfloat16).reshape(tok_count, experts, capacity)
    weights = numerators.astype(jnp.float32) / 128.0
    combine = (
        jnp.sum(placed * weights[:, :, None], axis=1)
        .astype(jnp.bfloat16)
        .reshape(tok_count, experts, capacity)
    )
    feature_halves = normed.reshape(tok_count, halves, half_width)
    outgoing = jnp.einsum(
        "tec,thf->ehcf", select, feature_halves, preferred_element_type=jnp.float32
    ).astype(jnp.bfloat16)
    arrived = lax.all_to_all(
        outgoing.reshape(experts * halves, capacity, half_width),
        ("grp", "loc"),
        split_axis=0,
        concat_axis=0,
        tiled=True,
    )
    expert_input = arrived.reshape(-1, half_width)
    gate_part = jnp.dot(expert_input, gate_weight[0], preferred_element_type=jnp.float32)
    up_part = jnp.dot(expert_input, up_weight[0], preferred_element_type=jnp.float32)
    down_local = down_weight[0]
    gate_sum, up_sum = (
        lax.psum(gate_part.astype(jnp.bfloat16), "loc").astype(jnp.float32),
        lax.psum(up_part.astype(jnp.bfloat16), "loc").astype(jnp.float32),
    )
    hidden_all = (jax.nn.silu(gate_sum) * up_sum).astype(jnp.bfloat16)
    expert_out = jnp.dot(hidden_all, down_local, preferred_element_type=jnp.float32)
    expert_out = expert_out.astype(jnp.bfloat16)
    returned = lax.all_to_all(
        expert_out.reshape(experts * halves, capacity, half_width),
        ("grp", "loc"),
        split_axis=0,
        concat_axis=0,
        tiled=True,
    ).reshape(experts, halves, capacity, half_width)
    mixed = jnp.einsum("tec,ehcf->thf", combine, returned, preferred_element_type=jnp.float32)
    return mixed.reshape(tok_count, width).astype(jnp.bfloat16)


def chain_kernel(
    lanes, steps, cap,
    tok_ref, gain_ref, ids_ref, num_ref, gate_hbm, up_hbm, down_hbm, out_ref,
    gate_w, up_w, down_w, stage, gathered, meta, cross, rows, part, part_in, made, back, total, total_in, last, last_in,
    weight_sem, pair_send, pair_recv, pair_meta_send, pair_meta_recv, hop_send, hop_recv, meta_send, meta_recv,
    cross_send, cross_recv, part_send, part_recv, back_send, back_recv, sum_send, sum_recv, last_send, last_recv,
):
    tok_count, width = tok_ref.shape
    half_width = width // 2
    hidden_width = gate_w.shape[1]
    experts = lanes * steps
    half_tok = tok_count // 2
    group = lax.axis_index("grp")
    core = lax.axis_index("loc")
    place = group // lanes
    lane = group % lanes
    other_core = 1 - core
    other_lane = place * lanes + 1 - lane
    left, right = group - lanes, group + lanes
    has_left, has_right = place > 0, place < steps - 1
    mesh_id = pl.DeviceIdType.MESH

    def remote(src, dst, send, recv, target):
        return pltpu.make_async_remote_copy(
            src_ref=src, dst_ref=dst, send_sem=send, recv_sem=recv, device_id=target, device_id_type=mesh_id
        )

    weight_copies = [
        pltpu.make_async_copy(src.at[0], dst, weight_sem.at[k])
        for k, (src, dst) in enumerate(((gate_hbm, gate_w), (up_hbm, up_w), (down_hbm, down_w)))
    ]
    for copy in weight_copies:
        copy.start()

    barrier = pltpu.get_barrier_semaphore()
    pl.semaphore_signal(barrier, inc=1, device_id={"loc": other_core}, device_id_type=mesh_id)
    pl.semaphore_signal(barrier, inc=1, device_id={"grp": other_lane}, device_id_type=mesh_id)

    @pl.when(has_left)
    def _():
        pl.semaphore_signal(barrier, inc=1, device_id={"grp": left}, device_id_type=mesh_id)

    @pl.when(has_right)
    def _():
        pl.semaphore_signal(barrier, inc=1, device_id={"grp": right}, device_id_type=mesh_id)

    expert_row = lax.broadcasted_iota(jnp.int32, (experts, tok_count), 0)
    named = jnp.zeros((experts, tok_count), jnp.float32)
    weight = jnp.zeros((experts, tok_count), jnp.float32)
    for k in range(ids_ref.shape[0]):
        hit = ids_ref[k : k + 1, :] == expert_row
        named = named + jnp.where(hit, 1.0, 0.0)
        weight = weight + jnp.where(hit, num_ref[k : k + 1, :].astype(jnp.float32) / 128.0, 0.0)
    earlier = lax.broadcasted_iota(jnp.int32, (tok_count, tok_count), 0) < lax.broadcasted_iota(
        jnp.int32, (tok_count, tok_count), 1
    )
    slot = jnp.dot(
        named.astype(jnp.bfloat16),
        jnp.where(earlier, 1.0, 0.0).astype(jnp.bfloat16),
        preferred_element_type=jnp.float32,
    )
    meta[place, core, 0:experts, :] = jnp.where(named > 0.5, slot, -1.0)
    meta[place, core, experts : 2 * experts, :] = weight

    values = tok_ref[...].astype(jnp.float32)
    scale = lax.rsqrt(jnp.mean(values * values, axis=-1, keepdims=True) + 1e-06)

    def normed(which):
        cols = pl.ds(pl.multiple_of(which * half_width, 128), half_width)
        return (tok_ref[:, cols].astype(jnp.float32) * scale * gain_ref[cols][None, :]).astype(jnp.bfloat16)

    stage[...] = normed(other_core)
    pl.semaphore_wait(barrier, 2 + has_left.astype(jnp.int32) + has_right.astype(jnp.int32))
    own = (place, core)
    pair_copies = [
        remote(stage, gathered.at[own], pair_send, pair_recv, {"loc": other_core}),
        remote(meta.at[own], meta.at[own], pair_meta_send, pair_meta_recv, {"loc": other_core}),
    ]
    for copy in pair_copies:
        copy.start()
    gathered[place, core] = normed(core)
    for copy in pair_copies:
        copy.wait_send()
    got = (place, other_core)
    remote(stage, gathered.at[got], pair_send, pair_recv, {"loc": other_core}).wait_recv()
    remote(meta.at[got], meta.at[got], pair_meta_send, pair_meta_recv, {"loc": other_core}).wait_recv()

    def hop(b, h, side, p):
        target = {"grp": (left, right)[side]}
        at = pl.ds(p * half_tok, half_tok)
        chunk_rows = gathered.at[b, h, at]
        copies = [remote(chunk_rows, chunk_rows, hop_send.at[side, b, h, p], hop_recv.at[b, h, p], target)]
        if p == 0:
            copies.append(
                remote(meta.at[b, h], meta.at[b, h], meta_send.at[side, b, h], meta_recv.at[b, h], target)
            )
        return copies

    def start_hop(b, h, side, p):
        for copy in hop(b, h, side, p):
            copy.start()

    def hop_of(i, upstream, sign):
        first = i <= upstream
        d = jnp.where(first, i, 2 * upstream + 1 - i)
        return d, place + sign * d, jnp.where(first, 0, 1)

    def forward(i):
        ways = ((steps - 1 - place, 1, 0, has_left), (place, -1, 1, has_right))
        for upstream, sign, side, has_next in ways:
            d, b, h = hop_of(i, upstream, sign)

            @pl.when((d == 0) & has_next)
            def _():
                for p in range(2):
                    start_hop(b, h, side, p)

        for p in range(2):
            for upstream, sign, side, has_next in ways:
                d, b, h = hop_of(i, upstream, sign)

                @pl.when(d > 0)
                def _():
                    for copy in hop(b, h, side, p):
                        copy.wait_recv()

                    @pl.when(has_next)
                    def _():
                        start_hop(b, h, side, p)

    def chunk(i):
        h = i // steps
        j = jnp.where(h == 0, i, 2 * steps - 1 - i)
        near = jnp.minimum(place, steps - 1 - place)
        both = j <= 2 * near
        d = jnp.where(both, (j + 1) // 2, j - near)
        up = jnp.where(both, j % 2 == 0, place < steps - 1 - place)
        return jnp.where(up, place + d, place - d), h

    slot_row = lax.broadcasted_iota(jnp.int32, (cap, tok_count), 0).astype(jnp.float32)

    def table(b, h, expert):
        return meta[b, h, pl.ds(expert, 1), :] == slot_row

    def weighted(b, h, expert):
        return jnp.where(table(b, h, expert), meta[b, h, pl.ds(experts + expert, 1), :], 0.0).astype(jnp.bfloat16)

    def pick(b, h, expert):
        chosen = jnp.where(table(b, h, expert), 1.0, 0.0).astype(jnp.bfloat16)
        return jnp.dot(chosen, gathered[b, h], preferred_element_type=jnp.float32).astype(jnp.bfloat16)

    def cross_copy(b, h):
        return remote(
            cross.at[b, h], rows.at[b, h, pl.ds(cap, cap)], cross_send.at[b, h], cross_recv.at[b, h], {"grp": other_lane}
        )

    def part_copy(b, h):
        return remote(part.at[b, h], part_in.at[b, h], part_send.at[b, h], part_recv.at[b, h], {"loc": other_core})

    def back_copy(b, h):
        return remote(
            made.at[b, h, pl.ds(cap, cap)], back.at[b, h], back_send.at[b, h], back_recv.at[b, h], {"grp": other_lane}
        )

    def sum_copy(b, h, side, p):
        at = pl.ds(p * half_tok, half_tok)
        return remote(
            total.at[b, h, at],
            total_in.at[side, b, h, at],
            sum_send.at[b, h, p],
            sum_recv.at[side, b, h, p],
            {"grp": (left, right)[side]},
        )

    def select(b, h):
        cross[b, h] = pick(b, h, other_lane)
        cross_copy(b, h).start()
        rows[b, h, 0:cap, :] = pick(b, h, group)

    def gate_up(b, h):
        cross_copy(b, h).wait_recv()
        for k, w in enumerate((gate_w, up_w)):
            part[b, h, :, k * hidden_width : (k + 1) * hidden_width] = jnp.dot(
                rows[b, h], w[...], preferred_element_type=jnp.float32
            ).astype(jnp.bfloat16)
        part_copy(b, h).start()

    def down(b, h):
        part_copy(b, h).wait_recv()
        both = part[b, h].astype(jnp.float32) + part_in[b, h].astype(jnp.float32)
        gate_sum, up_sum = both[:, :hidden_width], both[:, hidden_width:]
        hidden = (gate_sum / (1.0 + jnp.exp(-gate_sum)) * up_sum).astype(jnp.bfloat16)
        made[b, h] = jnp.dot(hidden, down_w[...], preferred_element_type=jnp.float32).astype(jnp.bfloat16)
        back_copy(b, h).start()

    def combine(b, h):
        back_copy(b, h).wait_recv()
        dims = (((0,), (0,)), ((), ()))
        total[b, h] = (
            lax.dot_general(weighted(b, h, group), made[b, h, 0:cap, :], dims, preferred_element_type=jnp.float32)
            + lax.dot_general(weighted(b, h, other_lane), back[b, h], dims, preferred_element_type=jnp.float32)
        ).astype(jnp.bfloat16)

        @pl.when((b > place) & jnp.logical_not(has_left))
        def _():
            for p in range(2):
                sum_copy(b, h, 1, p).start()

        @pl.when((b < place) & jnp.logical_not(has_right))
        def _():
            for p in range(2):
                sum_copy(b, h, 0, p).start()

    def add_in(b, h, side, p):
        sum_copy(b, h, side, p).wait_recv()
        at = pl.ds(p * half_tok, half_tok)
        total[b, h, at] = (
            total[b, h, at].astype(jnp.float32) + total_in[side, b, h, at].astype(jnp.float32)
        ).astype(jnp.bfloat16)

    def add_on(b, h, side):
        for p in range(2):
            add_in(b, h, side, p)
            sum_copy(b, h, side, p).start()

    def reduce_step(i):
        for h in range(2):
            since_right = i - 1 - 2 * place
            since_left = i - 1 - 2 * (steps - 1 - place)
            if h == 0:
                going_right, going_left = since_right, steps - 1 - since_left
            else:
                going_right, going_left = 2 * steps - 1 - since_right, since_left - steps

            @pl.when(has_left & (going_right > place) & (going_right < steps))
            def _():
                add_on(going_right, h, 1)

            @pl.when(has_right & (going_left < place) & (going_left >= 0))
            def _():
                add_on(going_left, h, 0)

    def body(i, carry):
        @pl.when(i < 2 * steps)
        def _():
            select(*chunk(i))

        @pl.when((i >= 1) & (i <= 2 * steps))
        def _():
            down(*chunk(i - 1))

        reduce_step(i)

        @pl.when(i == 0)
        def _():
            for copy in weight_copies:
                copy.wait()

        @pl.when(i < 2 * steps)
        def _():
            gate_up(*chunk(i))

        @pl.when(i + 1 < 2 * steps)
        def _():
            forward(i + 1)

        @pl.when((i >= 1) & (i <= 2 * steps))
        def _():
            combine(*chunk(i - 1))

        return carry

    forward(0)
    lax.fori_loop(0, max(3 * steps - 2, 2 * steps + 1), body, 0)

    def finish(h):
        @pl.when(has_left)
        def _():
            for p in range(2):
                add_in(place, h, 1, p)

        @pl.when(has_right)
        def _():
            for p in range(2):
                add_in(place, h, 0, p)

    last_copy = remote(last, last_in, last_send, last_recv, {"loc": other_core})
    for h in range(2):
        finish(h)

        @pl.when(h != core)
        def _():
            last[...] = total[place, h]
            last_copy.start()

        @pl.when(h == core)
        def _():
            out_ref[:, pl.ds(pl.multiple_of(core * half_width, 128), half_width)] = total[place, h]

    last_copy.wait()
    out_ref[:, pl.ds(pl.multiple_of(other_core * half_width, 128), half_width)] = last_in[...]

    def drain(i, carry):
        b, h = i // 2, i % 2

        @pl.when((b <= place) & has_right)
        def _():
            for p in range(2):
                for copy in hop(b, h, 1, p):
                    copy.wait_send()

        @pl.when((b >= place) & has_left)
        def _():
            for p in range(2):
                for copy in hop(b, h, 0, p):
                    copy.wait_send()

        cross_copy(b, h).wait_send()
        part_copy(b, h).wait_send()
        back_copy(b, h).wait_send()

        @pl.when(b != place)
        def _():
            for p in range(2):
                sum_copy(b, h, 0, p).wait_send()

        return carry

    lax.fori_loop(0, 2 * steps, drain, 0)


def chained(tokens, norm_gain, gate_weight, up_weight, down_weight, expert_ids, numerators):
    tok_count, width = tokens.shape
    experts = lax.axis_size("grp")
    half_width = width // 2
    hidden_width = gate_weight.shape[2]
    lanes = 2
    steps = experts // lanes
    cap = capacity_of(tok_count, experts)
    bf = jnp.bfloat16
    dma = pltpu.SemaphoreType.DMA
    vmem = pl.BlockSpec(memory_space=pltpu.VMEM)
    hbm = pl.BlockSpec(memory_space=pl.ANY)
    return pl.pallas_call(
        functools.partial(chain_kernel, lanes, steps, cap),
        out_shape=jax.ShapeDtypeStruct((tok_count, width), bf),
        in_specs=[vmem, vmem, vmem, vmem, hbm, hbm, hbm],
        out_specs=vmem,
        scratch_shapes=[
            pltpu.VMEM((half_width, hidden_width), bf),
            pltpu.VMEM((half_width, hidden_width), bf),
            pltpu.VMEM((hidden_width, half_width), bf),
            pltpu.VMEM((tok_count, half_width), bf),
            pltpu.VMEM((steps, 2, tok_count, half_width), bf),
            pltpu.VMEM((steps, 2, 2 * experts, tok_count), jnp.float32),
            pltpu.VMEM((steps, 2, cap, half_width), bf),
            pltpu.VMEM((steps, 2, 2 * cap, half_width), bf),
            pltpu.VMEM((steps, 2, 2 * cap, 2 * hidden_width), bf),
            pltpu.VMEM((steps, 2, 2 * cap, 2 * hidden_width), bf),
            pltpu.VMEM((steps, 2, 2 * cap, half_width), bf),
            pltpu.VMEM((steps, 2, cap, half_width), bf),
            pltpu.VMEM((steps, 2, tok_count, half_width), bf),
            pltpu.VMEM((2, steps, 2, tok_count, half_width), bf),
            pltpu.VMEM((tok_count, half_width), bf),
            pltpu.VMEM((tok_count, half_width), bf),
            dma((3,)),
            dma, dma, dma, dma,
            dma((2, steps, 2, 2)), dma((steps, 2, 2)), dma((2, steps, 2)), dma((steps, 2)),
            dma((steps, 2)), dma((steps, 2)), dma((steps, 2)), dma((steps, 2)),
            dma((steps, 2)), dma((steps, 2)), dma((steps, 2, 2)), dma((2, steps, 2, 2)),
            dma, dma,
        ],
        compiler_params=pltpu.CompilerParams(
            collective_id=0, has_side_effects=True, vmem_limit_bytes=60 * 1024 * 1024
        ),
    )(tokens, norm_gain, expert_ids.T, numerators.T, gate_weight, up_weight, down_weight)


def capacity_of(tok_count, experts):
    return tok_count // 2 - experts // 32 * (23 * tok_count // 64)


def solution(mesh):
    in_specs = (
        P(("rep", "grp", "loc"), None),
        P(),
        P("grp", "loc", None),
        P("grp", "loc", None),
        P("grp", None, "loc"),
        P(("rep", "grp", "loc"), None),
        P(("rep", "grp", "loc"), None),
    )
    out_specs = P(("rep", "grp", "loc"), None)
    experts, halves = mesh.shape["grp"], mesh.shape["loc"]

    def run(tokens, *rest):
        tok_count = tokens.shape[0] // mesh.size
        whole_tiles = capacity_of(tok_count, experts) % 16 == 0 and experts % 8 == 0 and halves == 2
        return jax.shard_map(
            chained if whole_tiles else local, mesh=mesh, in_specs=in_specs, out_specs=out_specs, check_vma=False
        )(tokens, *rest)

    return run
```
